32 devices in a mesh: groups: 2 (over x), expert: 8 (over z, y), dp: 2 (over core).
Axes of the slice: x: 2, y: 2, z: 4, core: 2. Of those that a mesh axis runs over, the one named last changes fastest.
Arguments:
- tokens: bfloat16 [4096, 2048], P(('groups', 'expert', 'dp')), parts along dimension 0, may hold values from -6 to 6
- expert_ids: int32 [4096, 8], P(('groups', 'expert', 'dp')), parts along dimension 0, may hold values from 0 to 31, all different within a row; in each aligned block of 128 rows (0 to 127, 128 to 255, ...) at most 40 rows name the same one
- logits: float32 [4096, 8], P(('groups', 'expert', 'dp')), parts along dimension 0
- cotangent: bfloat16 [4096, 2048], P(('groups', 'expert', 'dp')), parts along dimension 0, may hold values from -6 to 6
- w_gate: bfloat16 [32, 2048, 768], P(('expert', 'dp')), may hold values from -0.125 to 0.125
- w_up: bfloat16 [32, 2048, 768], P(('expert', 'dp')), may hold values from -0.125 to 0.125
- w_down: bfloat16 [32, 768, 2048], P(('expert', 'dp')), may hold values from -0.21875 to 0.21875
Outputs:
- mixed: bfloat16 [4096, 2048], P(('groups', 'expert', 'dp')), parts along dimension 0
- grad_tokens: bfloat16 [4096, 2048], P(('groups', 'expert', 'dp')), parts along dimension 0
- grad_logits: float32 [4096, 8], P(('groups', 'expert', 'dp')), parts along dimension 0
- grad_down: bfloat16 [64, 768, 2048], P(('groups', 'expert', 'dp')), parts along dimension 0
The draws below stay inside these ranges and needn't reach their ends.
There are 2 independent parts, one for each index of `groups`. The reference program is written for one: setup_inputs(seed, part) draws one part's arguments, and reference() takes and returns one part's arrays. A program takes and returns all parts, laid end to end along the dimension named above; an argument that names none is the same for every part. Nothing has to cross between parts.
Inputs may be any that keep to these rules, and one draw needn't show every extreme that they name: `expert_ids`: each row names 8 different experts; within the rows of one device no expert is named by more than 40 rows, a bound that some block reaches.
All inputs are finite; a program needn't handle non-finite values.
Results may differ from the reference program's by a relative error of at most 0.0064.
Values may be sent and summed in bfloat16 or wider, within the bound.
A program may use at most 192 MiB of HBM per device.

```python
import math
import jax
import jax.numpy as jnp
import numpy as np
from jax import lax

D = 2048
FF = 768
TOP = 8
TOK_DEV = 128
EXPERTS = 32
TOKENS = 2048
CAP = 40
N_EXPERT = 8
N_DP = 2


def draw_logits(key, part):
    key = jax.random.fold_in(key, 11)
    key_base = jax.random.fold_in(key, 0)
    return 1.5 * jax.random.normal(key_base, (TOKENS, TOP), jnp.float32)


def block_levels(stream_key, dims, pieces, least, top_value):
    loudness = 1.0
    for dim, blocks in pieces:
        steps = jax.random.uniform(jax.random.fold_in(jax.random.fold_in(stream_key, 6), dim), (blocks,), jnp.float32, least / len(pieces), top_value / len(pieces))
        loudness = loudness * jnp.repeat(jnp.exp(steps), dims[dim] // blocks).reshape((-1,) + (1,) * (len(dims) - 1 - dim))
    return loudness


def deal_out(stream_key, own, number, rows, count, top, bound, skew):
    sequence = jax.random.permutation(stream_key, count)
    crowded, ordinary = shares(count, rows * top, bound, skew, True), shares(count, rows * top, bound, skew, False)
    places = jnp.arange(count)

    def named(lengths, turn):
        used = int((lengths > 0).sum())
        fixed = max(1, used // 4)
        passed = fixed + (places - fixed + turn * (used - fixed)) % max(1, count - fixed)
        return jnp.zeros((count,), jnp.int32).at[sequence[jnp.where(places < fixed, places, passed)]].set(jnp.asarray(lengths, jnp.int32))

    lengths = jnp.where(number % 4 == 0, named(crowded, number // 4), named(ordinary, number - number // 4 - 1))
    mixed = jax.random.permutation(jax.random.fold_in(own, 3), count)
    source_of, sink = mixed[0:count // 2 * 2:2], mixed[1:count // 2 * 2:2]
    room = jnp.minimum(lengths[source_of] - 1, bound - lengths[sink]) // 2
    room = jnp.where((source_of == sequence[0]) | (sink == sequence[0]) | (lengths[sink] == 0), 0, jnp.maximum(room, 0))
    passed = jax.random.randint(jax.random.fold_in(own, 4), (count // 2,), 0, 1 << 20) % (room + 1)
    lengths = lengths.at[source_of].add(-passed).at[sink].add(passed)
    labels = jnp.searchsorted(jnp.cumsum(lengths), jnp.arange(rows * top), side="right").astype(jnp.int32)
    listing = labels.reshape(top, rows).T
    listing = listing[jax.random.permutation(jax.random.fold_in(own, 1), rows)]
    turn = jax.random.randint(jax.random.fold_in(own, 2), (rows, 1), 0, top)
    return jnp.take_along_axis(listing, (jnp.arange(top)[None, :] + turn) % top, axis=1)


def shares(count, total, most, lean, full):
    loads = [(1 << 20) // math.isqrt(rank ** lean) + 1 for rank in range(1, count + 1)]
    largest = most if full else min(most, max(-(-total // count), total * loads[0] // sum(loads)))
    least = 1 if total - largest >= count - 1 else 0
    given, surplus = [largest] + [least] * (count - 1), total - largest - least * (count - 1)
    while surplus > 0:
        free = [i for i in range(1, count) if given[i] < largest] or [i for i in range(1, count) if given[i] < most]
        pool, budget = sum([loads[i] for i in free]), surplus
        for i in free:
            addition = min(most - given[i], max(1, budget * loads[i] // pool), surplus)
            given[i] = given[i] + addition
            surplus = surplus - addition
    return np.array(given)


def normal_values(rng, shape, deviation, most, cuts=(), held_as=jnp.bfloat16):
    factor_of = block_levels(rng, shape, cuts, -0.22, 0.18) if cuts else 1.0
    entries = jax.random.normal(rng, shape, jnp.float32) * deviation * factor_of
    return jnp.minimum(jnp.maximum(entries, -most), most).astype(held_as)


def setup_inputs(seed: int = 0, part: int = 0) -> dict:
    keys = jax.random.split(jax.random.key(seed), 8)
    part_keys = jax.random.split(jax.random.fold_in(keys[7], part), 8)
    tokens = normal_values(part_keys[0], (TOKENS, D), 1.0, 6.0, ((0, 16),))
    expert_ids_keys = jax.random.split(jax.random.fold_in(part_keys[1], 1), TOKENS // TOK_DEV)
    expert_ids_turns = jax.random.permutation(jax.random.fold_in(part_keys[1], 3), TOKENS // TOK_DEV)
    expert_ids = jax.vmap(lambda own, number: deal_out(jax.random.fold_in(part_keys[1], 2), own, number, TOK_DEV, EXPERTS, TOP, CAP, 2))(expert_ids_keys, expert_ids_turns).reshape((TOKENS, TOP))
    logits = draw_logits(jax.random.fold_in(jax.random.fold_in(keys[7], part), 71), part)
    cotangent = normal_values(part_keys[3], (TOKENS, D), 1.0, 6.0, ((0, 16),))
    w_gate = normal_values(keys[4], (EXPERTS, D, FF), D ** -0.5, 0.125, ((0, 16),))
    w_up = normal_values(keys[5], (EXPERTS, D, FF), D ** -0.5, 0.125, ((0, 16),))
    w_down = normal_values(keys[6], (EXPERTS, FF, D), FF ** -0.5, 0.21875, ((0, 16),))
    return {"tokens": tokens, "expert_ids": expert_ids, "logits": logits, "cotangent": cotangent, "w_gate": w_gate, "w_up": w_up, "w_down": w_down}


def reference(tokens, expert_ids, logits, cotangent, w_gate, w_up, w_down):
    gate_probs = jax.nn.softmax(logits, axis=-1)
    chosen = expert_ids.reshape(-1).astype(jnp.int32)
    assign_total = chosen.shape[0]
    sorted_order = jnp.argsort(chosen, stable=True).astype(jnp.int32)
    counts = jnp.zeros((EXPERTS,), jnp.int32).at[chosen].add(1)
    starts = jnp.cumsum(counts) - counts
    most_rows = CAP * N_EXPERT * N_DP
    probs_flat = gate_probs.reshape(-1)

    def one_expert(packed_item):
        expert_index, weight_gate, weight_up, weight_down = packed_item
        steps_along = jnp.arange(most_rows, dtype=jnp.int32)
        position = starts[expert_index] + steps_along
        is_live = steps_along < counts[expert_index]
        assigned = sorted_order[jnp.clip(position, 0, assign_total - 1)]
        owner_token = assigned // TOP
        rows_in = jnp.where(is_live[:, None], tokens[owner_token], jnp.zeros((), jnp.bfloat16))
        scaled_cot = (probs_flat[assigned][:, None] * cotangent[owner_token].astype(jnp.float32)).astype(jnp.bfloat16)
        scaled_cot = jnp.where(is_live[:, None], scaled_cot, jnp.zeros((), jnp.bfloat16))
        gate_pre = jnp.dot(rows_in, weight_gate, preferred_element_type=jnp.float32)
        up_pre = jnp.dot(rows_in, weight_up, preferred_element_type=jnp.float32)
        sigmoid_gate = jax.nn.sigmoid(gate_pre)
        silu_gate = gate_pre * sigmoid_gate
        hidden = (silu_gate * up_pre).astype(jnp.bfloat16)
        expert_out = jnp.dot(hidden, weight_down, preferred_element_type=jnp.float32).astype(jnp.bfloat16)
        grad_hidden = jnp.dot(scaled_cot, weight_down.T, preferred_element_type=jnp.float32)
        grad_gate = (grad_hidden * up_pre * sigmoid_gate * (1.0 + gate_pre * (1.0 - sigmoid_gate))).astype(jnp.bfloat16)
        grad_up = (grad_hidden * silu_gate).astype(jnp.bfloat16)
        grad_input = (jnp.dot(grad_gate, weight_gate.T, preferred_element_type=jnp.float32)
                      + jnp.dot(grad_up, weight_up.T, preferred_element_type=jnp.float32)).astype(jnp.bfloat16)
        grad_weight = jnp.dot(hidden.T, scaled_cot, preferred_element_type=jnp.float32).astype(jnp.bfloat16)
        return assigned, is_live, expert_out, grad_input, grad_weight

    assigned_all, live_all, outs_all, inputs_all, grad_down = lax.map(
        one_expert, (jnp.arange(EXPERTS, dtype=jnp.int32), w_gate, w_up, w_down))
    flat_index = assigned_all.reshape(-1)
    live_flat = live_all.reshape(-1, 1)
    expert_out = jnp.zeros((assign_total, D), jnp.float32).at[flat_index].add(
        jnp.where(live_flat, outs_all.reshape(-1, D).astype(jnp.float32), 0.0))
    grad_input = jnp.zeros((assign_total, D), jnp.float32).at[flat_index].add(
        jnp.where(live_flat, inputs_all.reshape(-1, D).astype(jnp.float32), 0.0))
    expert_out = expert_out.reshape(TOKENS, TOP, D)
    grad_input = grad_input.reshape(TOKENS, TOP, D)
    mixed = jnp.sum(gate_probs[:, :, None] * expert_out, axis=1).astype(jnp.bfloat16)
    grad_tokens = jnp.sum(grad_input, axis=1).astype(jnp.bfloat16)
    inner = jnp.sum(cotangent.astype(jnp.float32)[:, None, :] * expert_out, axis=-1)
    grad_logits = gate_probs * (inner - jnp.sum(gate_probs * inner, axis=-1, keepdims=True))
    return mixed, grad_tokens, grad_logits, grad_down
```

```python
import functools

import jax
import jax.numpy as jnp
from jax import lax
from jax.experimental import pallas as pl
from jax.experimental.pallas import tpu as pltpu
from jax.sharding import PartitionSpec as P

BF16 = jnp.bfloat16
F32 = jnp.float32
LAST = (((1,), (1,)), ((), ()))
FIRST = (((0,), (0,)), ((), ()))
VMEM_LIMIT = 60 * 1024 * 1024


def dot(a, b, dims=(((1,), (0,)), ((), ()))):
    return lax.dot_general(a, b, dims, preferred_element_type=F32)


def one_hot(pos_ref, e, b, rows):
    pos = pos_ref[e, b]
    return lax.broadcasted_iota(jnp.int32, (rows, pos.shape[1]), 0) == pos


def gather_rows(e, all_ref, pos_ref, dest_ref, rows, in_buf, in_sem):
    blocks, span = pos_ref.shape[1], pos_ref.shape[3]

    def fetch(b):
        slot = lax.rem(b, 2)
        source = all_ref.at[pl.ds(pl.multiple_of(b * span, span), span), :]
        return pltpu.make_async_copy(source, in_buf.at[slot], in_sem.at[slot])

    fetch(jnp.int32(0)).start()

    def step(b, carry):
        @pl.when(b + 1 < blocks)
        def _():
            fetch(b + 1).start()

        fetch(b).wait()
        pick = one_hot(pos_ref, e, b, rows).astype(BF16)
        chosen = dot(pick, in_buf[lax.rem(b, 2)]).astype(BF16)
        dest_ref[pl.ds(pl.multiple_of(b * rows, 16), rows), :] = chosen
        return carry

    lax.fori_loop(0, blocks, step, 0)


def scatter_rows(pos_ref, rows_ref, out_ref, rows, out_buf, out_sem):
    experts, blocks, span = pos_ref.shape[0], pos_ref.shape[1], pos_ref.shape[3]

    def send(b):
        slot = lax.rem(b, 2)
        target = out_ref.at[pl.ds(pl.multiple_of(b * span, span), span), :]
        return pltpu.make_async_copy(out_buf.at[slot], target, out_sem.at[slot])

    def step(b, carry):
        @pl.when(b >= 2)
        def _():
            send(b - 2).wait()

        here = pl.ds(pl.multiple_of(b * rows, 16), rows)
        total = None
        for e in range(experts):
            pick = one_hot(pos_ref, e, b, rows).astype(BF16)
            part = dot(pick, rows_ref[e, here, :], FIRST)
            total = part if total is None else total + part
        out_buf[lax.rem(b, 2)] = total.astype(BF16)
        send(b).start()
        return carry

    lax.fori_loop(0, blocks, step, 0)
    for b in range(max(0, blocks - 2), blocks):
        send(jnp.int32(b)).wait()


def forward_kernel(rows, tok_ref, pos_ref, p_ref, wg_ref, wu_ref, wd_ref,
                   g_ref, u_ref, prow_ref, hp_ref, mix_ref, x_ref, o_ref,
                   in_buf, out_buf, in_sem, out_sem):
    e = pl.program_id(0)
    blocks = pos_ref.shape[1]
    width, ff = wg_ref.shape[1], wg_ref.shape[2]
    gather_rows(e, tok_ref, pos_ref, x_ref, rows, in_buf, in_sem)

    def weigh(b, carry):
        pick = one_hot(pos_ref, e, b, rows)
        prob = jnp.sum(jnp.where(pick, p_ref[e, b], 0.0), axis=1, keepdims=True)
        prow_ref[0, pl.ds(pl.multiple_of(b * rows, 16), rows), :] = jnp.broadcast_to(prob, (rows, 128))
        return carry

    lax.fori_loop(0, blocks, weigh, 0)
    prob = prow_ref[0, :, 0:1]
    tile = 256
    for f in range(ff // tile):
        cols = slice(f * tile, (f + 1) * tile)
        gate = dot(x_ref[...], wg_ref[0, :, cols])
        up = dot(x_ref[...], wu_ref[0, :, cols])
        g_ref[0, :, cols] = gate
        u_ref[0, :, cols] = up
        hidden = gate * jax.nn.sigmoid(gate) * up
        hp_ref[0, :, cols] = (prob * hidden).astype(BF16)

    def outputs(n, carry):
        cols = pl.ds(pl.multiple_of(n * 256, 256), 256)
        o_ref[e, :, cols] = dot(hp_ref[0], wd_ref[0, :, cols]).astype(BF16)
        return carry

    lax.fori_loop(0, width // 256, outputs, 0)

    @pl.when(e == pl.num_programs(0) - 1)
    def _():
        scatter_rows(pos_ref, o_ref, mix_ref, rows, out_buf, out_sem)


def backward_kernel(rows, all_experts, me_ref, cot_ref, pos_ref, g_ref, u_ref, prow_ref, wg_ref,
                    wu_ref, wd_ref, crow_ref, gt_ref, gg_ref, gu_ref, gi_ref,
                    in_buf, out_buf, in_sem, out_sem):
    e = pl.program_id(0)
    width, ff = wg_ref.shape[1], wg_ref.shape[2]
    gather_rows(e, cot_ref, pos_ref, crow_ref.at[0], rows, in_buf, in_sem)
    prob = prow_ref[0, :, 0:1]
    inner = jnp.zeros_like(prob)
    tile = 256
    for f in range(ff // tile):
        cols = slice(f * tile, (f + 1) * tile)
        raw = dot(crow_ref[0], wd_ref[0, cols, :], LAST)
        gate = g_ref[0, :, cols]
        up = u_ref[0, :, cols]
        sig = jax.nn.sigmoid(gate)
        silu = gate * sig
        inner = inner + jnp.sum(raw * (silu * up), axis=1, keepdims=True)
        grad = prob * raw
        gg_ref[:, cols] = (grad * up * sig * (1.0 + gate * (1.0 - sig))).astype(BF16)
        gu_ref[:, cols] = (grad * silu).astype(BF16)

    def inputs(n, carry):
        cols = pl.ds(pl.multiple_of(n * 256, 256), 256)
        total = dot(gg_ref[...], wg_ref[0, cols, :], LAST) + dot(gu_ref[...], wu_ref[0, cols, :], LAST)
        gi_ref[e, :, cols] = total.astype(BF16)
        return carry

    lax.fori_loop(0, width // 256, inputs, 0)
    extra = gi_ref.shape[2] - width
    high = inner.astype(BF16).astype(F32)
    low = inner - high
    lane = lax.broadcasted_iota(jnp.int32, (inner.shape[0], extra), 1)
    mine = me_ref[0] * pl.num_programs(0) + e
    packed = jnp.where(lane == mine, high, jnp.where(lane == mine + all_experts, low, 0.0))
    gi_ref[e, :, width:] = packed.astype(BF16)

    @pl.when(e == pl.num_programs(0) - 1)
    def _():
        scatter_rows(pos_ref, gi_ref, gt_ref, rows, out_buf, out_sem)


def whole(shape):
    return pl.BlockSpec(shape, lambda e: (0,) * len(shape), pipeline_mode=pl.Buffered(1))


def by_expert(shape):
    return pl.BlockSpec((1,) + shape[1:], lambda e: (e,) + (0,) * (len(shape) - 1))


def on_device(tokens, expert_ids, logits, cotangent, w_gate, w_up, w_down):
    axes = ("expert", "dp")
    tok_rows, width = tokens.shape
    top = expert_ids.shape[1]
    local, _, ff = w_gate.shape
    devices = lax.axis_size("expert") * lax.axis_size("dp")
    experts = local * devices
    capacity = 5 * tok_rows * top // (4 * experts)
    fold = max(1, 80 // capacity)
    rows, span, blocks = fold * capacity, fold * tok_rows, devices // fold
    all_rows = rows * blocks
    me = lax.axis_index(axes)

    every_tok = lax.all_gather(tokens, axes, axis=0, tiled=True)
    every_cot = lax.all_gather(cotangent, axes, axis=0, tiled=True)

    probs = jax.nn.softmax(logits, axis=-1)
    chosen = expert_ids[:, :, None] == jnp.arange(experts, dtype=jnp.int32)
    named = jnp.any(chosen, axis=1)
    dense = jnp.sum(jnp.where(chosen, probs[:, :, None], 0.0), axis=1)
    before = jnp.tril(jnp.ones((tok_rows, tok_rows), BF16), -1)
    rank = dot(before, named.astype(BF16))
    place = jnp.where(named, rank, -1000.0)
    small = lax.all_gather(jnp.concatenate([dense.T, place.T], axis=0), axes, axis=0, tiled=False)
    own_p = lax.dynamic_slice_in_dim(small, me * local, local, axis=1)
    own_pos = lax.dynamic_slice_in_dim(small, experts + me * local, local, axis=1)
    shift = (jnp.arange(devices) % fold * capacity).astype(F32)
    own_pos = (own_pos + shift[:, None, None]).astype(jnp.int32)
    own_p = own_p.transpose(1, 0, 2).reshape(local, blocks, 1, span)
    own_pos = own_pos.transpose(1, 0, 2).reshape(local, blocks, 1, span)

    params = pltpu.CompilerParams(vmem_limit_bytes=VMEM_LIMIT, dimension_semantics=("arbitrary",))
    unit = 2 * local * all_rows * width * ff
    f_shape, w_shape = (local, all_rows, ff), (local, width, ff)
    gate, up, prow, hp, mix = pl.pallas_call(
        functools.partial(forward_kernel, rows),
        grid=(local,),
        in_specs=[pl.BlockSpec(memory_space=pl.ANY), whole(own_pos.shape), whole(own_p.shape),
                  by_expert(w_gate.shape), by_expert(w_up.shape), by_expert(w_down.shape)],
        out_specs=[by_expert(f_shape), by_expert(f_shape), by_expert((local, all_rows, 128)),
                   by_expert(f_shape), pl.BlockSpec(memory_space=pl.ANY)],
        out_shape=[jax.ShapeDtypeStruct(f_shape, F32), jax.ShapeDtypeStruct(f_shape, F32),
                   jax.ShapeDtypeStruct((local, all_rows, 128), F32),
                   jax.ShapeDtypeStruct(f_shape, BF16),
                   jax.ShapeDtypeStruct((devices * tok_rows, width), BF16)],
        scratch_shapes=[pltpu.VMEM((all_rows, width), BF16),
                        pltpu.VMEM((local, all_rows, width), BF16),
                        pltpu.VMEM((2, span, width), BF16), pltpu.VMEM((2, span, width), BF16),
                        pltpu.SemaphoreType.DMA((2,)), pltpu.SemaphoreType.DMA((2,))],
        compiler_params=params,
        cost_estimate=pl.CostEstimate(flops=3 * unit, bytes_accessed=40 << 20, transcendentals=0),
        name="forward",
    )(every_tok, own_pos, own_p, w_gate, w_up, w_down)
    mixed = lax.psum_scatter(mix, axes, scatter_dimension=0, tiled=True)

    extra = -(-2 * experts // 128) * 128
    crow, gt = pl.pallas_call(
        functools.partial(backward_kernel, rows, experts),
        grid=(local,),
        in_specs=[pl.BlockSpec(memory_space=pltpu.SMEM), pl.BlockSpec(memory_space=pl.ANY), whole(own_pos.shape),
                  by_expert(f_shape), by_expert(f_shape), by_expert((local, all_rows, 128)),
                  by_expert(w_gate.shape), by_expert(w_up.shape), by_expert(w_down.shape)],
        out_specs=[by_expert((local, all_rows, width)), pl.BlockSpec(memory_space=pl.ANY)],
        out_shape=[jax.ShapeDtypeStruct((local, all_rows, width), BF16),
                   jax.ShapeDtypeStruct((devices * tok_rows, width + extra), BF16)],
        scratch_shapes=[pltpu.VMEM((all_rows, ff), BF16), pltpu.VMEM((all_rows, ff), BF16),
                        pltpu.VMEM((local, all_rows, width + extra), BF16),
                        pltpu.VMEM((2, span, width), BF16), pltpu.VMEM((2, span, width + extra), BF16),
                        pltpu.SemaphoreType.DMA((2,)), pltpu.SemaphoreType.DMA((2,))],
        compiler_params=params,
        cost_estimate=pl.CostEstimate(flops=3 * unit, bytes_accessed=40 << 20, transcendentals=0),
        name="backward",
    )(me.reshape(1).astype(jnp.int32), every_cot, own_pos, gate, up, prow, w_gate, w_up, w_down)
    gt, mixed = lax.optimization_barrier((gt, mixed))
    summed = lax.psum_scatter(gt, axes, scatter_dimension=0, tiled=True)

    grad_down = jnp.einsum("erf,erd->efd", hp, crow, preferred_element_type=F32).astype(BF16)
    grad_tokens = summed[:, :width]
    tail = summed[:, width:].astype(F32)
    products = tail[:, :experts] + tail[:, experts : 2 * experts]
    inner = jnp.sum(jnp.where(chosen, products[:, None, :], 0.0), axis=-1)
    grad_logits = probs * (inner - jnp.sum(probs * inner, axis=-1, keepdims=True))
    return (mixed, grad_tokens, grad_logits, grad_down)


def solution(mesh):
    rows = P(("groups", "expert", "dp"), None)
    weights = P(("expert", "dp"), None, None)
    return jax.shard_map(
        on_device,
        mesh=mesh,
        in_specs=(rows, rows, rows, rows, weights, weights, weights),
        out_specs=(rows, rows, rows, P(("groups", "expert", "dp"), None, None)),
        check_vma=False,
    )
```

```python
import functools

import jax
import jax.numpy as jnp
from jax import lax
from jax.experimental import pallas as pl
from jax.experimental.pallas import tpu as pltpu
from jax.sharding import PartitionSpec as P

BF16 = jnp.bfloat16
F32 = jnp.float32
LAST = (((1,), (1,)), ((), ()))
FIRST = (((0,), (0,)), ((), ()))
VMEM_LIMIT = 60 * 1024 * 1024


def dot(a, b, dims=(((1,), (0,)), ((), ()))):
    return lax.dot_general(a, b, dims, preferred_element_type=F32)


def one_hot(pos_ref, e, b, rows):
    pos = pos_ref[e, b]
    return lax.broadcasted_iota(jnp.int32, (rows, pos.shape[1]), 0) == pos


def gather_rows(e, all_ref, pos_ref, dest_ref, rows, in_buf, in_sem):
    blocks, span = pos_ref.shape[1], pos_ref.shape[3]

    def fetch(b):
        slot = lax.rem(b, 2)
        source = all_ref.at[pl.ds(pl.multiple_of(b * span, span), span), :]
        return pltpu.make_async_copy(source, in_buf.at[slot], in_sem.at[slot])

    fetch(jnp.int32(0)).start()

    def step(b, carry):
        @pl.when(b + 1 < blocks)
        def _():
            fetch(b + 1).start()

        fetch(b).wait()
        pick = one_hot(pos_ref, e, b, rows).astype(BF16)
        chosen = dot(pick, in_buf[lax.rem(b, 2)]).astype(BF16)
        dest_ref[pl.ds(pl.multiple_of(b * rows, 16), rows), :] = chosen
        return carry

    lax.fori_loop(0, blocks, step, 0)


def scatter_rows(pos_ref, rows_ref, out_ref, rows, out_buf, out_sem):
    experts, blocks, span = pos_ref.shape[0], pos_ref.shape[1], pos_ref.shape[3]

    def send(b):
        slot = lax.rem(b, 2)
        target = out_ref.at[pl.ds(pl.multiple_of(b * span, span), span), :]
        return pltpu.make_async_copy(out_buf.at[slot], target, out_sem.at[slot])

    def step(b, carry):
        @pl.when(b >= 2)
        def _():
            send(b - 2).wait()

        here = pl.ds(pl.multiple_of(b * rows, 16), rows)
        total = None
        for e in range(experts):
            pick = one_hot(pos_ref, e, b, rows).astype(BF16)
            part = dot(pick, rows_ref[e, here, :], FIRST)
            total = part if total is None else total + part
        out_buf[lax.rem(b, 2)] = total.astype(BF16)
        send(b).start()
        return carry

    lax.fori_loop(0, blocks, step, 0)
    for b in range(max(0, blocks - 2), blocks):
        send(jnp.int32(b)).wait()


def forward_kernel(rows, tok_ref, pos_ref, p_ref, wg_ref, wu_ref, wd_ref,
                   g_ref, u_ref, prow_ref, hp_ref, mix_ref, x_ref, o_ref,
                   in_buf, out_buf, in_sem, out_sem):
    e = pl.program_id(0)
    blocks = pos_ref.shape[1]
    width, ff = wg_ref.shape[1], wg_ref.shape[2]
    gather_rows(e, tok_ref, pos_ref, x_ref, rows, in_buf, in_sem)

    def weigh(b, carry):
        pick = one_hot(pos_ref, e, b, rows)
        prob = jnp.sum(jnp.where(pick, p_ref[e, b], 0.0), axis=1, keepdims=True)
        prow_ref[0, pl.ds(pl.multiple_of(b * rows, 16), rows), :] = jnp.broadcast_to(prob, (rows, 128))
        return carry

    lax.fori_loop(0, blocks, weigh, 0)
    prob = prow_ref[0, :, 0:1]
    tile = 256
    for f in range(ff // tile):
        cols = slice(f * tile, (f + 1) * tile)
        gate = dot(x_ref[...], wg_ref[0, :, cols])
        up = dot(x_ref[...], wu_ref[0, :, cols])
        g_ref[0, :, cols] = gate
        u_ref[0, :, cols] = up
        hidden = gate * jax.nn.sigmoid(gate) * up
        hp_ref[0, :, cols] = (prob * hidden).astype(BF16)

    def outputs(n, carry):
        cols = pl.ds(pl.multiple_of(n * 256, 256), 256)
        o_ref[e, :, cols] = dot(hp_ref[0], wd_ref[0, :, cols]).astype(BF16)
        return carry

    lax.fori_loop(0, width // 256, outputs, 0)

    @pl.when(e == pl.num_programs(0) - 1)
    def _():
        scatter_rows(pos_ref, o_ref, mix_ref, rows, out_buf, out_sem)


def backward_kernel(rows, all_experts, me_ref, cot_ref, pos_ref, g_ref, u_ref, prow_ref, wg_ref,
                    wu_ref, wd_ref, crow_ref, gt_ref, gg_ref, gu_ref, gi_ref,
                    in_buf, out_buf, in_sem, out_sem):
    e = pl.program_id(0)
    width, ff = wg_ref.shape[1], wg_ref.shape[2]
    gather_rows(e, cot_ref, pos_ref, crow_ref.at[0], rows, in_buf, in_sem)
    prob = prow_ref[0, :, 0:1]
    inner = jnp.zeros_like(prob)
    tile = 256
    for f in range(ff // tile):
        cols = slice(f * tile, (f + 1) * tile)
        raw = dot(crow_ref[0], wd_ref[0, cols, :], LAST)
        gate = g_ref[0, :, cols]
        up = u_ref[0, :, cols]
        sig = jax.nn.sigmoid(gate)
        silu = gate * sig
        inner = inner + jnp.sum(raw * (silu * up), axis=1, keepdims=True)
        grad = prob * raw
        gg_ref[:, cols] = (grad * up * sig * (1.0 + gate * (1.0 - sig))).astype(BF16)
        gu_ref[:, cols] = (grad * silu).astype(BF16)

    def inputs(n, carry):
        cols = pl.ds(pl.multiple_of(n * 256, 256), 256)
        total = dot(gg_ref[...], wg_ref[0, cols, :], LAST) + dot(gu_ref[...], wu_ref[0, cols, :], LAST)
        gi_ref[e, :, cols] = total.astype(BF16)
        return carry

    lax.fori_loop(0, width // 256, inputs, 0)
    extra = gi_ref.shape[2] - width
    high = inner.astype(BF16).astype(F32)
    low = inner - high
    lane = lax.broadcasted_iota(jnp.int32, (inner.shape[0], extra), 1)
    mine = me_ref[0] * pl.num_programs(0) + e
    packed = jnp.where(lane == mine, high, jnp.where(lane == mine + all_experts, low, 0.0))
    gi_ref[e, :, width:] = packed.astype(BF16)

    @pl.when(e == pl.num_programs(0) - 1)
    def _():
        scatter_rows(pos_ref, gi_ref, gt_ref, rows, out_buf, out_sem)


def whole(shape):
    return pl.BlockSpec(shape, lambda e: (0,) * len(shape), pipeline_mode=pl.Buffered(1))


def by_expert(shape):
    return pl.BlockSpec((1,) + shape[1:], lambda e: (e,) + (0,) * (len(shape) - 1))


def ring_place(index, n):
    odd = index % 2
    return (1 - odd) * (index // 2) + odd * (n - 1 - index // 2)


def ring_index(place, n):
    place = (place + 2 * n) % n
    back = place // (n // 2)
    return (1 - back) * (2 * place) + back * (2 * (n - 1 - place) + 1)


def ring_hops(n):
    return [(d, c, n // 2 - (d != c)) for c in range(2) for d in range(2)]


def ring_setup(n):
    me, side = lax.axis_index("expert"), lax.axis_index("dp")
    place = ring_place(me, n)
    ahead = [{"expert": ring_index(place + 1, n)}, {"expert": ring_index(place - 1, n)}]
    sibling = {"dp": 1 - side}
    barrier = pltpu.get_barrier_semaphore()
    for other in ahead + [sibling]:
        pl.semaphore_signal(barrier, inc=1, device_id=other, device_id_type=pl.DeviceIdType.MESH)
    pl.semaphore_wait(barrier, 3)
    return me, side, place, ahead, sibling


def remote(source, target, send_sem, recv_sem, device):
    return pltpu.make_async_remote_copy(
        src_ref=source, dst_ref=target, send_sem=send_sem, recv_sem=recv_sem,
        device_id=device, device_id_type=pl.DeviceIdType.MESH)


def ring_gather_kernel(n, x_ref, out_ref, own_sem, send_sem, recv_sem, give_sem, take_sem, pair_sem):
    me, side, place, ahead, sibling = ring_setup(n)
    size = x_ref.shape[0]
    part = size // 2
    steps = [1, -1]

    def area(dp, index, c):
        start = pl.multiple_of((dp * n + index) * size + c * part, part)
        return out_ref.at[pl.ds(start, part), :]

    mine = out_ref.at[pl.ds(pl.multiple_of((side * n + me) * size, size), size), :]
    other = out_ref.at[pl.ds(pl.multiple_of(((1 - side) * n + me) * size, size), size), :]
    started = []
    chains = ring_hops(n)
    for d, c, hops in chains:
        copy = remote(x_ref.at[c * part : (c + 1) * part, :], area(side, me, c),
                      send_sem.at[d, c, 0], recv_sem.at[d, c, 0], ahead[d])
        copy.start()
        started.append(copy)
    local = pltpu.make_async_copy(x_ref, mine, own_sem)
    local.start()
    copy = remote(x_ref, mine, pair_sem.at[0], pair_sem.at[1], sibling)
    copy.start()
    started.append(copy)
    for s in range(n // 2):
        for d, c, hops in chains:
            if s >= hops:
                continue
            here = area(side, ring_index(place - steps[d] * (s + 1), n), c)
            remote(here, here, send_sem.at[d, c, s], recv_sem.at[d, c, s], ahead[d]).wait_recv()
            if s + 1 < hops:
                copy = remote(here, here, send_sem.at[d, c, s + 1], recv_sem.at[d, c, s + 1], ahead[d])
                copy.start()
                started.append(copy)
            copy = remote(here, here, give_sem.at[d, c, s], take_sem.at[d, c, s], sibling)
            copy.start()
            started.append(copy)
    for d, c, hops in chains:
        for s in range(hops):
            here = area(1 - side, ring_index(place - steps[d] * (s + 1), n), c)
            remote(here, here, give_sem.at[d, c, s], take_sem.at[d, c, s], sibling).wait_recv()
    remote(x_ref, other, pair_sem.at[0], pair_sem.at[1], sibling).wait_recv()
    for copy in started:
        copy.wait_send()
    local.wait()


def ring_gather(block):
    n = lax.axis_size("expert")
    size, width = block.shape
    sems = pltpu.SemaphoreType.DMA((2, 2, n // 2))
    return pl.pallas_call(
        functools.partial(ring_gather_kernel, n),
        in_specs=[pl.BlockSpec(memory_space=pl.ANY)],
        out_specs=pl.BlockSpec(memory_space=pl.ANY),
        out_shape=jax.ShapeDtypeStruct((2 * n * size, width), block.dtype),
        scratch_shapes=[pltpu.SemaphoreType.DMA, sems, sems, sems, sems, pltpu.SemaphoreType.DMA((2,))],
        compiler_params=pltpu.CompilerParams(collective_id=0, has_side_effects=True),
        name="ring_gather",
    )(block)


def ring_scatter_kernel(n, parts_ref, out_ref, sib_ref, load_ref, land_ref,
                        give_sem, take_sem, send_sem, recv_sem):
    me, side, place, ahead, sibling = ring_setup(n)
    size = out_ref.shape[0]
    part = size // 2
    steps = [1, -1]
    chains = ring_hops(n)

    def rows(dp, off, c, count):
        start = (dp * n + ring_index(place + off, n)) * size + c * part
        return pl.ds(pl.multiple_of(start, part), count)

    started = []
    offsets = [n // 2]
    for k in range(n // 2 - 1, 0, -1):
        offsets += [k, n - k]
    offsets.append(0)
    for off in offsets:
        copy = remote(parts_ref.at[rows(1 - side, off, 0, size), :], sib_ref.at[off],
                      give_sem.at[off], take_sem.at[off], sibling)
        copy.start()
        started.append(copy)
    ready = set()

    def own(off, c):
        off = off % n
        if off not in ready:
            ready.add(off)
            remote(sib_ref.at[off], sib_ref.at[off], give_sem.at[off], take_sem.at[off], sibling).wait_recv()
        return (parts_ref[rows(side, off, c, part), :].astype(F32)
                + sib_ref[off, c * part : (c + 1) * part, :].astype(F32))

    def arrived(d, c, s):
        slot = land_ref.at[d, c, s]
        remote(slot, slot, send_sem.at[d, c, s], recv_sem.at[d, c, s], ahead[d]).wait_recv()
        return land_ref[d, c, s].astype(F32)

    for s in range(n // 2):
        for d, c, hops in chains:
            if s >= hops:
                continue
            total = own(steps[d] * (hops - s), c)
            if s > 0:
                total = total + arrived(d, c, s - 1)
            load_ref[d, c, s] = total.astype(load_ref.dtype)
            copy = remote(load_ref.at[d, c, s], land_ref.at[d, c, s],
                          send_sem.at[d, c, s], recv_sem.at[d, c, s], ahead[d])
            copy.start()
            started.append(copy)
    for c in range(2):
        total = own(0, c)
        for d, half, hops in chains:
            if half == c:
                total = total + arrived(d, c, hops - 1)
        out_ref[c * part : (c + 1) * part, :] = total.astype(out_ref.dtype)
    for copy in started:
        copy.wait_send()


def ring_scatter(parts):
    n = lax.axis_size("expert")
    all_rows, width = parts.shape
    size = all_rows // (2 * n)
    sems = pltpu.SemaphoreType.DMA((2, 2, n // 2))
    slots = pltpu.VMEM((2, 2, n // 2, size // 2, width), parts.dtype)
    return pl.pallas_call(
        functools.partial(ring_scatter_kernel, n),
        in_specs=[pl.BlockSpec(memory_space=pltpu.VMEM)],
        out_specs=pl.BlockSpec(memory_space=pltpu.VMEM),
        out_shape=jax.ShapeDtypeStruct((size, width), parts.dtype),
        scratch_shapes=[pltpu.VMEM((n, size, width), parts.dtype), slots, slots,
                        pltpu.SemaphoreType.DMA((n,)), pltpu.SemaphoreType.DMA((n,)), sems, sems],
        compiler_params=pltpu.CompilerParams(
            collective_id=1, has_side_effects=True, vmem_limit_bytes=VMEM_LIMIT),
        name="ring_scatter",
    )(parts)


def on_device(tokens, expert_ids, logits, cotangent, w_gate, w_up, w_down):
    axes = ("expert", "dp")
    tok_rows, width = tokens.shape
    top = expert_ids.shape[1]
    local, _, ff = w_gate.shape
    devices = lax.axis_size("expert") * lax.axis_size("dp")
    experts = local * devices
    capacity = 5 * tok_rows * top // (4 * experts)
    fold = max(1, 80 // capacity)
    rows, span, blocks = fold * capacity, fold * tok_rows, devices // fold
    all_rows = rows * blocks
    me = lax.axis_index(axes)

    every_cot = lax.all_gather(cotangent, ("dp", "expert"), axis=0, tiled=True)

    probs = jax.nn.softmax(logits, axis=-1)
    chosen = expert_ids[:, :, None] == jnp.arange(experts, dtype=jnp.int32)
    named = jnp.any(chosen, axis=1)
    dense = jnp.sum(jnp.where(chosen, probs[:, :, None], 0.0), axis=1)
    before = jnp.tril(jnp.ones((tok_rows, tok_rows), BF16), -1)
    rank = dot(before, named.astype(BF16))
    place = jnp.where(named, rank, -1000.0)
    small = lax.all_gather(jnp.concatenate([dense.T, place.T], axis=0), ("dp", "expert"), axis=0, tiled=False)
    tokens, small = lax.optimization_barrier((tokens, small))
    every_tok = ring_gather(tokens)
    own_p = lax.dynamic_slice_in_dim(small, me * local, local, axis=1)
    own_pos = lax.dynamic_slice_in_dim(small, experts + me * local, local, axis=1)
    shift = (jnp.arange(devices) % fold * capacity).astype(F32)
    own_pos = (own_pos + shift[:, None, None]).astype(jnp.int32)
    own_p = own_p.transpose(1, 0, 2).reshape(local, blocks, 1, span)
    own_pos = own_pos.transpose(1, 0, 2).reshape(local, blocks, 1, span)

    params = pltpu.CompilerParams(vmem_limit_bytes=VMEM_LIMIT, dimension_semantics=("arbitrary",))
    unit = 2 * local * all_rows * width * ff
    f_shape, w_shape = (local, all_rows, ff), (local, width, ff)
    gate, up, prow, hp, mix = pl.pallas_call(
        functools.partial(forward_kernel, rows),
        grid=(local,),
        in_specs=[pl.BlockSpec(memory_space=pl.ANY), whole(own_pos.shape), whole(own_p.shape),
                  by_expert(w_gate.shape), by_expert(w_up.shape), by_expert(w_down.shape)],
        out_specs=[by_expert(f_shape), by_expert(f_shape), by_expert((local, all_rows, 128)),
                   by_expert(f_shape), pl.BlockSpec(memory_space=pl.ANY)],
        out_shape=[jax.ShapeDtypeStruct(f_shape, F32), jax.ShapeDtypeStruct(f_shape, F32),
                   jax.ShapeDtypeStruct((local, all_rows, 128), F32),
                   jax.ShapeDtypeStruct(f_shape, BF16),
                   jax.ShapeDtypeStruct((devices * tok_rows, width), BF16)],
        scratch_shapes=[pltpu.VMEM((all_rows, width), BF16),
                        pltpu.VMEM((local, all_rows, width), BF16),
                        pltpu.VMEM((2, span, width), BF16), pltpu.VMEM((2, span, width), BF16),
                        pltpu.SemaphoreType.DMA((2,)), pltpu.SemaphoreType.DMA((2,))],
        compiler_params=params,
        cost_estimate=pl.CostEstimate(flops=3 * unit, bytes_accessed=40 << 20, transcendentals=0),
        name="forward",
    )(every_tok, own_pos, own_p, w_gate, w_up, w_down)
    mixed = lax.psum_scatter(mix, ("dp", "expert"), scatter_dimension=0, tiled=True)

    extra = -(-2 * experts // 128) * 128
    crow, gt = pl.pallas_call(
        functools.partial(backward_kernel, rows, experts),
        grid=(local,),
        in_specs=[pl.BlockSpec(memory_space=pltpu.SMEM), pl.BlockSpec(memory_space=pl.ANY), whole(own_pos.shape),
                  by_expert(f_shape), by_expert(f_shape), by_expert((local, all_rows, 128)),
                  by_expert(w_gate.shape), by_expert(w_up.shape), by_expert(w_down.shape)],
        out_specs=[by_expert((local, all_rows, width)), pl.BlockSpec(memory_space=pl.ANY)],
        out_shape=[jax.ShapeDtypeStruct((local, all_rows, width), BF16),
                   jax.ShapeDtypeStruct((devices * tok_rows, width + extra), BF16)],
        scratch_shapes=[pltpu.VMEM((all_rows, ff), BF16), pltpu.VMEM((all_rows, ff), BF16),
                        pltpu.VMEM((local, all_rows, width + extra), BF16),
                        pltpu.VMEM((2, span, width), BF16), pltpu.VMEM((2, span, width + extra), BF16),
                        pltpu.SemaphoreType.DMA((2,)), pltpu.SemaphoreType.DMA((2,))],
        compiler_params=params,
        cost_estimate=pl.CostEstimate(flops=3 * unit, bytes_accessed=40 << 20, transcendentals=0),
        name="backward",
    )(me.reshape(1).astype(jnp.int32), every_cot, own_pos, gate, up, prow, w_gate, w_up, w_down)
    summed = ring_scatter(gt)

    grad_down = jnp.einsum("erf,erd->efd", hp, crow, preferred_element_type=F32).astype(BF16)
    grad_tokens = summed[:, :width]
    tail = summed[:, width:].astype(F32)
    products = tail[:, :experts] + tail[:, experts : 2 * experts]
    inner = jnp.sum(jnp.where(chosen, products[:, None, :], 0.0), axis=-1)
    grad_logits = probs * (inner - jnp.sum(probs * inner, axis=-1, keepdims=True))
    return (mixed, grad_tokens, grad_logits, grad_down)


def solution(mesh):
    rows = P(("groups", "expert", "dp"), None)
    weights = P(("expert", "dp"), None, None)
    return jax.shard_map(
        on_device,
        mesh=mesh,
        in_specs=(rows, rows, rows, rows, weights, weights, weights),
        out_specs=(rows, rows, rows, P(("groups", "expert", "dp"), None, None)),
        check_vma=False,
    )
```

```python
import functools

import jax
import jax.numpy as jnp
from jax import lax
from jax.experimental import pallas as pl
from jax.experimental.pallas import tpu as pltpu
from jax.sharding import PartitionSpec as P

BF16 = jnp.bfloat16
F32 = jnp.float32
LAST = (((1,), (1,)), ((), ()))
FIRST = (((0,), (0,)), ((), ()))
VMEM_LIMIT = 60 * 1024 * 1024


def dot(a, b, dims=(((1,), (0,)), ((), ()))):
    return lax.dot_general(a, b, dims, preferred_element_type=F32)


def one_hot(pos_ref, e, b, rows):
    pos = pos_ref[e, b]
    return lax.broadcasted_iota(jnp.int32, (rows, pos.shape[1]), 0) == pos


def gather_rows(e, all_ref, pos_ref, dest_ref, rows, in_buf, in_sem):
    blocks, span = pos_ref.shape[1], pos_ref.shape[3]

    def fetch(b):
        slot = lax.rem(b, 2)
        source = all_ref.at[pl.ds(pl.multiple_of(b * span, span), span), 0 : in_buf.shape[2]]
        return pltpu.make_async_copy(source, in_buf.at[slot], in_sem.at[slot])

    fetch(jnp.int32(0)).start()

    def step(b, carry):
        @pl.when(b + 1 < blocks)
        def _():
            fetch(b + 1).start()

        fetch(b).wait()
        pick = one_hot(pos_ref, e, b, rows).astype(BF16)
        chosen = dot(pick, in_buf[lax.rem(b, 2)]).astype(BF16)
        dest_ref[pl.ds(pl.multiple_of(b * rows, 16), rows), :] = chosen
        return carry

    lax.fori_loop(0, blocks, step, 0)


def scatter_rows(pos_ref, rows_ref, out_ref, rows, out_buf, out_sem):
    experts, blocks, span = pos_ref.shape[0], pos_ref.shape[1], pos_ref.shape[3]

    def send(b):
        slot = lax.rem(b, 2)
        target = out_ref.at[pl.ds(pl.multiple_of(b * span, span), span), :]
        return pltpu.make_async_copy(out_buf.at[slot], target, out_sem.at[slot])

    def step(b, carry):
        @pl.when(b >= 2)
        def _():
            send(b - 2).wait()

        here = pl.ds(pl.multiple_of(b * rows, 16), rows)
        total = None
        for e in range(experts):
            pick = one_hot(pos_ref, e, b, rows).astype(BF16)
            part = dot(pick, rows_ref[e, here, :], FIRST)
            total = part if total is None else total + part
        out_buf[lax.rem(b, 2)] = total.astype(BF16)
        send(b).start()
        return carry

    lax.fori_loop(0, blocks, step, 0)
    for b in range(max(0, blocks - 2), blocks):
        send(jnp.int32(b)).wait()


def forward_kernel(rows, tok_ref, pos_ref, p_ref, wg_ref, wu_ref, wd_ref,
                   g_ref, u_ref, prow_ref, hp_ref, mix_ref, x_ref, o_ref,
                   in_buf, out_buf, in_sem, out_sem):
    e = pl.program_id(0)
    blocks = pos_ref.shape[1]
    width, ff = wg_ref.shape[1], wg_ref.shape[2]
    gather_rows(e, tok_ref, pos_ref, x_ref, rows, in_buf, in_sem)

    def weigh(b, carry):
        pick = one_hot(pos_ref, e, b, rows)
        prob = jnp.sum(jnp.where(pick, p_ref[e, b], 0.0), axis=1, keepdims=True)
        prow_ref[0, pl.ds(pl.multiple_of(b * rows, 16), rows), :] = jnp.broadcast_to(prob, (rows, 128))
        return carry

    lax.fori_loop(0, blocks, weigh, 0)
    prob = prow_ref[0, :, 0:1]
    tile = 256
    for f in range(ff // tile):
        cols = slice(f * tile, (f + 1) * tile)
        gate = dot(x_ref[...], wg_ref[0, :, cols])
        up = dot(x_ref[...], wu_ref[0, :, cols])
        g_ref[0, :, cols] = gate
        u_ref[0, :, cols] = up
        hidden = gate * jax.nn.sigmoid(gate) * up
        hp_ref[0, :, cols] = (prob * hidden).astype(BF16)

    def outputs(n, carry):
        cols = pl.ds(pl.multiple_of(n * 256, 256), 256)
        o_ref[e, :, cols] = dot(hp_ref[0], wd_ref[0, :, cols]).astype(BF16)
        return carry

    lax.fori_loop(0, width // 256, outputs, 0)

    @pl.when(e == pl.num_programs(0) - 1)
    def _():
        scatter_rows(pos_ref, o_ref, mix_ref, rows, out_buf, out_sem)


def backward_kernel(rows, all_experts, me_ref, cot_ref, pos_ref, g_ref, u_ref, prow_ref, wg_ref,
                    wu_ref, wd_ref, crow_ref, gt_ref, gg_ref, gu_ref, gi_ref,
                    in_buf, out_buf, in_sem, out_sem):
    e = pl.program_id(0)
    width, ff = wg_ref.shape[1], wg_ref.shape[2]
    gather_rows(e, cot_ref, pos_ref, crow_ref.at[0], rows, in_buf, in_sem)
    prob = prow_ref[0, :, 0:1]
    inner = jnp.zeros_like(prob)
    tile = 256
    for f in range(ff // tile):
        cols = slice(f * tile, (f + 1) * tile)
        raw = dot(crow_ref[0], wd_ref[0, cols, :], LAST)
        gate = g_ref[0, :, cols]
        up = u_ref[0, :, cols]
        sig = jax.nn.sigmoid(gate)
        silu = gate * sig
        inner = inner + jnp.sum(raw * (silu * up), axis=1, keepdims=True)
        grad = prob * raw
        gg_ref[:, cols] = (grad * up * sig * (1.0 + gate * (1.0 - sig))).astype(BF16)
        gu_ref[:, cols] = (grad * silu).astype(BF16)

    def inputs(n, carry):
        cols = pl.ds(pl.multiple_of(n * 256, 256), 256)
        total = dot(gg_ref[...], wg_ref[0, cols, :], LAST) + dot(gu_ref[...], wu_ref[0, cols, :], LAST)
        gi_ref[e, :, cols] = total.astype(BF16)
        return carry

    lax.fori_loop(0, width // 256, inputs, 0)
    extra = gi_ref.shape[2] - width
    high = inner.astype(BF16).astype(F32)
    low = inner - high
    lane = lax.broadcasted_iota(jnp.int32, (inner.shape[0], extra), 1)
    mine = me_ref[0] * pl.num_programs(0) + e
    packed = jnp.where(lane == mine, high, jnp.where(lane == mine + all_experts, low, 0.0))
    gi_ref[e, :, width:] = packed.astype(BF16)

    @pl.when(e == pl.num_programs(0) - 1)
    def _():
        scatter_rows(pos_ref, gi_ref, gt_ref, rows, out_buf, out_sem)


def whole(shape):
    return pl.BlockSpec(shape, lambda e: (0,) * len(shape), pipeline_mode=pl.Buffered(1))


def by_expert(shape):
    return pl.BlockSpec((1,) + shape[1:], lambda e: (e,) + (0,) * (len(shape) - 1))


def ring_place(index, n):
    odd = index % 2
    return (1 - odd) * (index // 2) + odd * (n - 1 - index // 2)


def ring_index(place, n):
    place = (place + 2 * n) % n
    back = place // (n // 2)
    return (1 - back) * (2 * place) + back * (2 * (n - 1 - place) + 1)


def ring_hops(n):
    return [(d, c, n // 2 - (d != c)) for c in range(2) for d in range(2)]


def ring_setup(n):
    me, side = lax.axis_index("expert"), lax.axis_index("dp")
    place = ring_place(me, n)
    ahead = [{"expert": ring_index(place + 1, n)}, {"expert": ring_index(place - 1, n)}]
    sibling = {"dp": 1 - side}
    barrier = pltpu.get_barrier_semaphore()
    for other in ahead + [sibling]:
        pl.semaphore_signal(barrier, inc=1, device_id=other, device_id_type=pl.DeviceIdType.MESH)
    pl.semaphore_wait(barrier, 3)
    return me, side, place, ahead, sibling


def remote(source, target, send_sem, recv_sem, device):
    return pltpu.make_async_remote_copy(
        src_ref=source, dst_ref=target, send_sem=send_sem, recv_sem=recv_sem,
        device_id=device, device_id_type=pl.DeviceIdType.MESH)


def ring_gather_kernel(n, x_ref, out_ref, own_sem, send_sem, recv_sem, give_sem, take_sem, pair_sem):
    me, side, place, ahead, sibling = ring_setup(n)
    size = x_ref.shape[0]
    part = size // 2
    steps = [1, -1]

    def area(dp, index, c):
        start = pl.multiple_of((dp * n + index) * size + c * part, part)
        return out_ref.at[pl.ds(start, part), :]

    mine = out_ref.at[pl.ds(pl.multiple_of((side * n + me) * size, size), size), :]
    other = out_ref.at[pl.ds(pl.multiple_of(((1 - side) * n + me) * size, size), size), :]
    started = []
    chains = ring_hops(n)
    for d, c, hops in chains:
        copy = remote(x_ref.at[c * part : (c + 1) * part, :], area(side, me, c),
                      send_sem.at[d, c, 0], recv_sem.at[d, c, 0], ahead[d])
        copy.start()
        started.append(copy)
    local = pltpu.make_async_copy(x_ref, mine, own_sem)
    local.start()
    copy = remote(x_ref, mine, pair_sem.at[0], pair_sem.at[1], sibling)
    copy.start()
    started.append(copy)
    for s in range(n // 2):
        for d, c, hops in chains:
            if s >= hops:
                continue
            here = area(side, ring_index(place - steps[d] * (s + 1), n), c)
            remote(here, here, send_sem.at[d, c, s], recv_sem.at[d, c, s], ahead[d]).wait_recv()
            if s + 1 < hops:
                copy = remote(here, here, send_sem.at[d, c, s + 1], recv_sem.at[d, c, s + 1], ahead[d])
                copy.start()
                started.append(copy)
            copy = remote(here, here, give_sem.at[d, c, s], take_sem.at[d, c, s], sibling)
            copy.start()
            started.append(copy)
    for d, c, hops in chains:
        for s in range(hops):
            here = area(1 - side, ring_index(place - steps[d] * (s + 1), n), c)
            remote(here, here, give_sem.at[d, c, s], take_sem.at[d, c, s], sibling).wait_recv()
    remote(x_ref, other, pair_sem.at[0], pair_sem.at[1], sibling).wait_recv()
    for copy in started:
        copy.wait_send()
    local.wait()


def ring_gather(block):
    n = lax.axis_size("expert")
    size, width = block.shape
    sems = pltpu.SemaphoreType.DMA((2, 2, n // 2))
    return pl.pallas_call(
        functools.partial(ring_gather_kernel, n),
        in_specs=[pl.BlockSpec(memory_space=pl.ANY)],
        out_specs=pl.BlockSpec(memory_space=pl.ANY),
        out_shape=jax.ShapeDtypeStruct((2 * n * size, width), block.dtype),
        scratch_shapes=[pltpu.SemaphoreType.DMA, sems, sems, sems, sems, pltpu.SemaphoreType.DMA((2,))],
        compiler_params=pltpu.CompilerParams(collective_id=0, has_side_effects=True),
        name="ring_gather",
    )(block)


def ring_scatter_kernel(n, parts_ref, out_ref, sib_ref, load_ref, land_ref,
                        give_sem, take_sem, send_sem, recv_sem):
    me, side, place, ahead, sibling = ring_setup(n)
    size = out_ref.shape[0]
    part = size // 2
    steps = [1, -1]
    chains = ring_hops(n)

    def rows(dp, off, c, count):
        start = (dp * n + ring_index(place + off, n)) * size + c * part
        return pl.ds(pl.multiple_of(start, part), count)

    started = []
    offsets = [n // 2]
    for k in range(n // 2 - 1, 0, -1):
        offsets += [k, n - k]
    offsets.append(0)
    for off in offsets:
        copy = remote(parts_ref.at[rows(1 - side, off, 0, size), :], sib_ref.at[off],
                      give_sem.at[off], take_sem.at[off], sibling)
        copy.start()
        started.append(copy)
    ready = set()

    def own(off, c):
        off = off % n
        if off not in ready:
            ready.add(off)
            remote(sib_ref.at[off], sib_ref.at[off], give_sem.at[off], take_sem.at[off], sibling).wait_recv()
        return (parts_ref[rows(side, off, c, part), :].astype(F32)
                + sib_ref[off, c * part : (c + 1) * part, :].astype(F32))

    def arrived(d, c, s):
        slot = land_ref.at[d, c, s]
        remote(slot, slot, send_sem.at[d, c, s], recv_sem.at[d, c, s], ahead[d]).wait_recv()
        return land_ref[d, c, s].astype(F32)

    for s in range(n // 2):
        for d, c, hops in chains:
            if s >= hops:
                continue
            total = own(steps[d] * (hops - s), c)
            if s > 0:
                total = total + arrived(d, c, s - 1)
            load_ref[d, c, s] = total.astype(load_ref.dtype)
            copy = remote(load_ref.at[d, c, s], land_ref.at[d, c, s],
                          send_sem.at[d, c, s], recv_sem.at[d, c, s], ahead[d])
            copy.start()
            started.append(copy)
    for c in range(2):
        total = own(0, c)
        for d, half, hops in chains:
            if half == c:
                total = total + arrived(d, c, hops - 1)
        out_ref[c * part : (c + 1) * part, :] = total.astype(out_ref.dtype)
    for copy in started:
        copy.wait_send()


def ring_scatter(parts):
    n = lax.axis_size("expert")
    all_rows, width = parts.shape
    size = all_rows // (2 * n)
    sems = pltpu.SemaphoreType.DMA((2, 2, n // 2))
    slots = pltpu.VMEM((2, 2, n // 2, size // 2, width), parts.dtype)
    return pl.pallas_call(
        functools.partial(ring_scatter_kernel, n),
        in_specs=[pl.BlockSpec(memory_space=pltpu.VMEM)],
        out_specs=pl.BlockSpec(memory_space=pltpu.VMEM),
        out_shape=jax.ShapeDtypeStruct((size, width), parts.dtype),
        scratch_shapes=[pltpu.VMEM((n, size, width), parts.dtype), slots, slots,
                        pltpu.SemaphoreType.DMA((n,)), pltpu.SemaphoreType.DMA((n,)), sems, sems],
        compiler_params=pltpu.CompilerParams(
            collective_id=1, has_side_effects=True, vmem_limit_bytes=VMEM_LIMIT),
        name="ring_scatter",
    )(parts)


def on_device(tokens, expert_ids, logits, cotangent, w_gate, w_up, w_down):
    axes = ("expert", "dp")
    tok_rows, width = tokens.shape
    top = expert_ids.shape[1]
    local, _, ff = w_gate.shape
    devices = lax.axis_size("expert") * lax.axis_size("dp")
    experts = local * devices
    capacity = 5 * tok_rows * top // (4 * experts)
    fold = max(1, 80 // capacity)
    rows, span, blocks = fold * capacity, fold * tok_rows, devices // fold
    all_rows = rows * blocks
    me = lax.axis_index(axes)

    every_cot = lax.all_gather(cotangent, ("dp", "expert"), axis=0, tiled=True)

    probs = jax.nn.softmax(logits, axis=-1)
    chosen = expert_ids[:, :, None] == jnp.arange(experts, dtype=jnp.int32)
    named = jnp.any(chosen, axis=1)
    dense = jnp.sum(jnp.where(chosen, probs[:, :, None], 0.0), axis=1)
    before = jnp.tril(jnp.ones((tok_rows, tok_rows), BF16), -1)
    rank = dot(before, named.astype(BF16))
    place = jnp.where(named, rank, -1000.0)
    high = lax.reduce_precision(dense, 8, 7)
    notes = jnp.concatenate([high, dense - high, place], axis=1)
    notes = jnp.pad(notes, ((0, 0), (0, -3 * experts % 128))).astype(BF16)
    every_tok = ring_gather(jnp.concatenate([tokens, notes], axis=1))
    tail = every_tok[:, width:].astype(F32)
    own = [lax.dynamic_slice_in_dim(tail, k * experts + me * local, local, axis=1) for k in range(3)]
    shift = (jnp.arange(devices * tok_rows) // tok_rows % fold * capacity).astype(F32)
    own_p = (own[0] + own[1]).T.reshape(local, blocks, 1, span)
    own_pos = (own[2] + shift[:, None]).astype(jnp.int32).T.reshape(local, blocks, 1, span)

    params = pltpu.CompilerParams(vmem_limit_bytes=VMEM_LIMIT, dimension_semantics=("arbitrary",))
    unit = 2 * local * all_rows * width * ff
    f_shape, w_shape = (local, all_rows, ff), (local, width, ff)
    gate, up, prow, hp, mix = pl.pallas_call(
        functools.partial(forward_kernel, rows),
        grid=(local,),
        in_specs=[pl.BlockSpec(memory_space=pl.ANY), whole(own_pos.shape), whole(own_p.shape),
                  by_expert(w_gate.shape), by_expert(w_up.shape), by_expert(w_down.shape)],
        out_specs=[by_expert(f_shape), by_expert(f_shape), by_expert((local, all_rows, 128)),
                   by_expert(f_shape), pl.BlockSpec(memory_space=pl.ANY)],
        out_shape=[jax.ShapeDtypeStruct(f_shape, F32), jax.ShapeDtypeStruct(f_shape, F32),
                   jax.ShapeDtypeStruct((local, all_rows, 128), F32),
                   jax.ShapeDtypeStruct(f_shape, BF16),
                   jax.ShapeDtypeStruct((devices * tok_rows, width), BF16)],
        scratch_shapes=[pltpu.VMEM((all_rows, width), BF16),
                        pltpu.VMEM((local, all_rows, width), BF16),
                        pltpu.VMEM((2, span, width), BF16), pltpu.VMEM((2, span, width), BF16),
                        pltpu.SemaphoreType.DMA((2,)), pltpu.SemaphoreType.DMA((2,))],
        compiler_params=params,
        cost_estimate=pl.CostEstimate(flops=3 * unit, bytes_accessed=40 << 20, transcendentals=0),
        name="forward",
    )(every_tok, own_pos, own_p, w_gate, w_up, w_down)
    mixed = lax.psum_scatter(mix, ("dp", "expert"), scatter_dimension=0, tiled=True)

    extra = -(-2 * experts // 128) * 128
    crow, gt = pl.pallas_call(
        functools.partial(backward_kernel, rows, experts),
        grid=(local,),
        in_specs=[pl.BlockSpec(memory_space=pltpu.SMEM), pl.BlockSpec(memory_space=pl.ANY), whole(own_pos.shape),
                  by_expert(f_shape), by_expert(f_shape), by_expert((local, all_rows, 128)),
                  by_expert(w_gate.shape), by_expert(w_up.shape), by_expert(w_down.shape)],
        out_specs=[by_expert((local, all_rows, width)), pl.BlockSpec(memory_space=pl.ANY)],
        out_shape=[jax.ShapeDtypeStruct((local, all_rows, width), BF16),
                   jax.ShapeDtypeStruct((devices * tok_rows, width + extra), BF16)],
        scratch_shapes=[pltpu.VMEM((all_rows, ff), BF16), pltpu.VMEM((all_rows, ff), BF16),
                        pltpu.VMEM((local, all_rows, width + extra), BF16),
                        pltpu.VMEM((2, span, width), BF16), pltpu.VMEM((2, span, width + extra), BF16),
                        pltpu.SemaphoreType.DMA((2,)), pltpu.SemaphoreType.DMA((2,))],
        compiler_params=params,
        cost_estimate=pl.CostEstimate(flops=3 * unit, bytes_accessed=40 << 20, transcendentals=0),
        name="backward",
    )(me.reshape(1).astype(jnp.int32), every_cot, own_pos, gate, up, prow, w_gate, w_up, w_down)
    summed = ring_scatter(gt)

    grad_down = jnp.einsum("erf,erd->efd", hp, crow, preferred_element_type=F32).astype(BF16)
    grad_tokens = summed[:, :width]
    tail = summed[:, width:].astype(F32)
    products = tail[:, :experts] + tail[:, experts : 2 * experts]
    inner = jnp.sum(jnp.where(chosen, products[:, None, :], 0.0), axis=-1)
    grad_logits = probs * (inner - jnp.sum(probs * inner, axis=-1, keepdims=True))
    return (mixed, grad_tokens, grad_logits, grad_down)


def solution(mesh):
    rows = P(("groups", "expert", "dp"), None)
    weights = P(("expert", "dp"), None, None)
    return jax.shard_map(
        on_device,
        mesh=mesh,
        in_specs=(rows, rows, rows, rows, weights, weights, weights),
        out_specs=(rows, rows, rows, P(("groups", "expert", "dp"), None, None)),
        check_vma=False,
    )
```
